128 devices in a mesh: blk: 32 (over x_lo, z, y), rep: 4 (over x_hi, core).
Axes of the slice: x: 4 (x_hi: 2, x_lo: 2; x = x_hi * 2 + x_lo), y: 4, z: 4, core: 2. Of those that a mesh axis runs over, the one named last changes fastest.
Arguments:
- embeddings: bfloat16 [65536, 1024], P(('blk', 'rep')), as said below
- doc_ids: int32 [65536], P(('blk', 'rep')), may hold values from 0 to 32767, as said below
- plan: int32 [4, 32], replicated, may hold values from 0 to 31, as said below
Outputs:
- soft_score: float32 [65536], P(('blk', 'rep'))
The draws below stay inside these ranges and needn't reach their ends.
Inputs may be any that keep to these rules, and one draw needn't show every extreme that they name: plan[r, b] = b XOR m_r, with 4 distinct nonzero round values m_r; so block b meets plan[r, b] and that block meets b in round r. `doc_ids`: each id names exactly two rows of the cluster. `embeddings`: no row is zero.
All inputs are finite; a program needn't handle non-finite values.
Results may differ from the reference program's by a relative error of at most 0.0008.
Values may be sent and summed in bfloat16 or wider, within the bound.
A program may use at most 128 MiB of HBM per device.

```python
import jax
import jax.numpy as jnp
from jax import lax

D = 1024
ROUNDS = 4
INV_TEMP = 256
BLOCKS = 32
ROWS_BLK = 2048
N_DOC = 65536


def twin_ids(key):
    return (jax.random.permutation(jax.random.fold_in(key, 5), N_DOC) // 2).astype(jnp.int32)


def draw_doc_ids(key, part):
    return twin_ids(key)


def draw_embeddings(key, part):
    ids = twin_ids(key)
    key = jax.random.fold_in(key, 3)
    base = jax.random.normal(jax.random.fold_in(key, 0), (N_DOC, D), jnp.float32)
    table = jax.random.normal(jax.random.fold_in(key, 1), (N_DOC // 2, D), jnp.float32)
    rough = 0.4 * base + jnp.take(table, ids, axis=0)
    return rough.astype(jnp.bfloat16)


def draw_plan(key, part):
    key = jax.random.fold_in(key, 11)
    round_masks = (jax.random.permutation(key, BLOCKS - 1)[:ROUNDS] + 1).astype(jnp.int32)
    block_numbers = jnp.arange(BLOCKS, dtype=jnp.int32)
    return jnp.bitwise_xor(block_numbers[None, :], round_masks[:, None]).astype(jnp.int32)


def setup_inputs(seed: int = 0) -> dict:
    streams_of = jax.random.split(jax.random.key(seed), 4)
    embeddings = draw_embeddings(jax.random.fold_in(streams_of[3], 71), 0)
    doc_ids = draw_doc_ids(jax.random.fold_in(streams_of[3], 71), 0)
    plan = draw_plan(jax.random.fold_in(streams_of[3], 71), 0)
    return dict(embeddings=embeddings, doc_ids=doc_ids, plan=plan)


NEG = -1e+30

def normalize_rows(embeddings):
    widened = embeddings.astype(jnp.float32)
    return (widened * lax.rsqrt(lax.optimization_barrier(jnp.sum(widened * widened, axis=1, keepdims=True)) + 1e-06)).astype(jnp.bfloat16)

def reference(embeddings, doc_ids, plan):
    unit_rows = normalize_rows(embeddings)
    blocks = unit_rows.reshape(BLOCKS, ROWS_BLK, D)
    id_blocks = doc_ids.reshape(BLOCKS, ROWS_BLK)

    def one_block(index):
        own_rows = blocks[index]
        own_ids = id_blocks[index]

        def one_round(carry, round_index):
            partner = plan[round_index, index]
            scores = jnp.dot(own_rows, blocks[partner].T, preferred_element_type=jnp.float32) * INV_TEMP
            same_doc = own_ids[:, None] == id_blocks[partner][None, :]
            scores = jnp.where(same_doc, NEG, scores)
            row_top = lax.optimization_barrier(jnp.max(scores, axis=1))
            row_sum = lax.optimization_barrier(jnp.sum(jnp.where(same_doc, 0.0, jnp.exp(scores - row_top[:, None])), axis=1))
            best = jnp.maximum(carry[0], row_top)
            return ((best, carry[1] * jnp.exp(carry[0] - best) + row_sum * jnp.exp(row_top - best)), None)
        start_state = (jnp.full((ROWS_BLK,), NEG, jnp.float32), jnp.zeros((ROWS_BLK,), jnp.float32))
        (best, sum_exp), unused = lax.scan(one_round, start_state, jnp.arange(ROUNDS, dtype=jnp.int32))
        return (best + jnp.log(sum_exp)) / INV_TEMP
    return lax.map(one_block, jnp.arange(BLOCKS, dtype=jnp.int32)).reshape(N_DOC)
```

```python
import math

import jax
import jax.numpy as jnp
from jax import lax
from jax.experimental import pallas as pl
from jax.experimental.pallas import tpu as pltpu
from jax.sharding import PartitionSpec as P

MESH = pl.DeviceIdType.MESH
NEG = -1e30
SCALE = 256.0 * math.log2(math.e)
UNSCALE = math.log(2.0) / 256.0
ROWS = 512
SPOTS = 16
CHUNK = 32
HALF = 16
D = 1024
PARTS = 4


def lowest_bit(value):
    return jnp.bitwise_and(value, -value)


def odd_bits(value):
    value = jnp.bitwise_xor(value, jnp.right_shift(value, 4))
    value = jnp.bitwise_xor(value, jnp.right_shift(value, 2))
    value = jnp.bitwise_xor(value, jnp.right_shift(value, 1))
    return jnp.bitwise_and(value, 1)


def chooser(first, second):
    common = jnp.bitwise_and(first, second)
    return jnp.where(
        common != 0,
        lowest_bit(common),
        jnp.bitwise_or(lowest_bit(first), lowest_bit(second)),
    )


def kernel(
    plan,
    emb,
    ids,
    out,
    left,
    held,
    outbox,
    right,
    left_ids,
    id_in,
    id_table,
    scores,
    row_max,
    row_sum,
    row_in,
    col_own,
    col_in,
    col_table,
    one_s,
    one_r,
    rep_s,
    rep_r,
    two_s,
    two_r,
    own_s,
    own_r,
    ida_s,
    ida_r,
    idb_s,
    idb_r,
    row_s,
    row_r,
    cola_s,
    cola_r,
    colb_s,
    colb_r,
):
    blk = lax.axis_index("blk")
    rep = lax.axis_index("rep")
    lo, z, y = blk // 16, (blk // 4) % 4, blk % 4
    hi, core = rep // 2, rep % 2
    here = z * 4 + y

    def at_spot(k):
        return (lo * 16 + ((z + k // 4) % 4) * 4 + (y + k % 4) % 4, rep)

    def spot_to(k):
        return ((z + k // 4) % 4) * 4 + (y + k % 4) % 4

    def spot_from(k):
        return ((z + 4 - k // 4) % 4) * 4 + (y + 4 - k % 4) % 4

    intra = ((1 - lo) * 16 + here, rep)
    inter = ((1 - lo) * 16 + here, (1 - hi) * 2 + core)
    sibling = (blk, hi * 2 + 1 - core)
    across = (blk, (1 - hi) * 2 + core)
    diagonal = (blk, (1 - hi) * 2 + 1 - core)

    def remote(src, dst, send, recv, device):
        return pltpu.make_async_remote_copy(
            src_ref=src,
            dst_ref=dst,
            send_sem=send,
            recv_sem=recv,
            device_id=device,
            device_id_type=MESH,
        )

    def loop(first, last, body):
        def step(k, carry):
            body(k)
            return carry

        lax.fori_loop(first, last, step, jnp.int32(0))

    barrier = pltpu.get_barrier_semaphore()
    for device in (intra, inter, sibling, across, diagonal):
        pl.semaphore_signal(barrier, inc=1, device_id=device, device_id_type=MESH)
    loop(
        1,
        SPOTS,
        lambda k: pl.semaphore_signal(barrier, inc=1, device_id=at_spot(k), device_id_type=MESH),
    )

    def normalize(i):
        rows = pl.ds(pl.multiple_of(i * 64, 64), 64)
        wide = emb[rows, :].astype(jnp.float32)
        total = jnp.sum(wide * wide, axis=1, keepdims=True)
        left[0, rows, :] = (wide * lax.rsqrt(total + 1e-06)).astype(jnp.bfloat16)

    loop(0, ROWS // 64, normalize)
    id_in[0, 0:4, :] = ids[...]
    id_in[0, 4:8, :] = ids[...]
    pl.semaphore_wait(barrier, SPOTS - 1 + 5)

    def spread(k):
        rows = pl.ds(pl.multiple_of(spot_to(k) * CHUNK, CHUNK), CHUNK)
        return remote(
            left.at[0, rows], held.at[0, here], one_s.at[k], one_r.at[k], at_spot(k)
        )

    loop(1, SPOTS, lambda k: spread(k).start())
    held[0, here] = left[0, pl.ds(pl.multiple_of(here * CHUNK, CHUNK), CHUNK), :]

    group = (sibling, across, diagonal, intra, inter)

    def id_copy(j):
        return remote(id_in.at[0], id_in.at[j], ida_s.at[j], ida_r.at[j], group[j - 1])

    for j in range(1, 6):
        id_copy(j).start()

    def to_sibling():
        return remote(left.at[0], left.at[1], own_s.at[0], own_r.at[0], sibling)

    def to_across(i):
        rows = pl.ds(i * (ROWS // PARTS), ROWS // PARTS)
        return remote(
            left.at[0, rows], left.at[2, rows], own_s.at[1 + i], own_r.at[1 + i], across
        )

    def forward(i):
        rows = pl.ds(i * (ROWS // PARTS), ROWS // PARTS)
        j = 1 + PARTS + i
        return remote(left.at[2, rows], left.at[3, rows], own_s.at[j], own_r.at[j], sibling)

    to_sibling().start()
    to_across(0).start()

    def hand(k, side):
        rows = pl.ds(side * HALF, HALF)
        spot = spot_from(k)
        return remote(
            held.at[0, spot, rows],
            held.at[1, spot, rows],
            rep_s.at[side, k],
            rep_r.at[side, k],
            (intra, inter)[side],
        )

    hand(0, 0).start()
    hand(0, 1).start()

    def pass_on(k):
        spread(k).wait_recv()
        hand(k, 0).start()
        hand(k, 1).start()

    loop(1, SPOTS, pass_on)
    for i in range(1, PARTS):
        to_across(i).start()

    for j in range(1, 6):
        id_copy(j).wait_recv()
    lane = lax.broadcasted_iota(jnp.int32, (8, 128), 1)
    first_half = lane % CHUNK < HALF
    beside = jnp.where(first_half, id_in[4], id_in[5])
    id_table[here, 0:4, :] = id_in[0, 0:4, :]
    id_table[here, 4:8, :] = beside[0:4, :]

    def id_spread(k):
        return remote(
            id_table.at[here], id_table.at[here], idb_s.at[k], idb_r.at[k], at_spot(k)
        )

    loop(1, SPOTS, lambda k: id_spread(k).start())

    masks = [plan[r, 0] for r in range(4)]
    choosers = [chooser(masks[0], masks[1]), chooser(masks[2], masks[3])]

    def hosted_mask(pair, block):
        second = odd_bits(jnp.bitwise_and(block, choosers[pair]))
        return jnp.where(second == 1, masks[2 * pair + 1], masks[2 * pair])

    def guest_mask(pair, block):
        second = odd_bits(jnp.bitwise_and(block, choosers[pair]))
        return jnp.where(second == 1, masks[2 * pair], masks[2 * pair + 1])

    def place(mask, spot):
        return jnp.right_shift(mask, 4), jnp.bitwise_xor(spot, jnp.bitwise_and(mask, 15))

    def drain(k):
        hand(k, 0).wait_recv()
        hand(k, 1).wait_recv()

    loop(0, SPOTS, drain)

    def deliver(pair, k):
        return remote(
            outbox.at[pair, k],
            right.at[pair, here],
            two_s.at[pair, k],
            two_r.at[pair, k],
            at_spot(k),
        )

    for pair in range(2):

        def send_rows(k, pair=pair):
            spot = spot_to(k)
            side, source = place(hosted_mask(pair, lo * 16 + spot), spot)
            outbox[pair, k] = held[side, source]
            deliver(pair, k).start()

        loop(1, SPOTS, send_rows)
        side, source = place(hosted_mask(pair, blk), here)
        right[pair, here] = held[side, source]

    for j in range(4):
        for g in range(4):
            wide_ids = jnp.broadcast_to(id_in[j, g : g + 1, :], (128, 128))
            left_ids[pl.ds(j * ROWS + g * 128, 128), :] = wide_ids.T

    loop(1, SPOTS, lambda k: id_spread(k).wait_recv())

    def tile(pair, slot, right_ids, state):
        scores[...] = lax.dot_general(
            left[slot],
            right[pair].reshape(ROWS, D),
            (((1,), (1,)), ((), ())),
            preferred_element_type=jnp.float32,
        )

        def step(i, state):
            tops, sums = state
            rows = pl.ds(pl.multiple_of(i * 64, 64), 64)
            base = pl.ds(pl.multiple_of(slot * ROWS + i * 64, 64), 64)
            own_ids = left_ids[base, :]
            values = []
            for g in range(4):
                part = scores[rows, g * 128 : (g + 1) * 128] * SCALE
                values.append(jnp.where(own_ids == right_ids[g : g + 1, :], NEG, part))
            top = jnp.maximum(
                jnp.maximum(values[0], values[1]), jnp.maximum(values[2], values[3])
            )
            row_max[pair, base, :] = top
            row_sum[pair, base, :] = (
                jnp.exp2(values[0] - top)
                + jnp.exp2(values[1] - top)
                + jnp.exp2(values[2] - top)
                + jnp.exp2(values[3] - top)
            )
            new_tops, new_sums = [], []
            for g in range(4):
                stack = values[g].reshape(8, 8, 128)
                new = jnp.maximum(tops[g], jnp.max(stack, axis=0))
                new_tops.append(new)
                new_sums.append(
                    sums[g] * jnp.exp2(tops[g] - new)
                    + jnp.sum(jnp.exp2(stack - new[None]), axis=0)
                )
            return tuple(new_tops), tuple(new_sums)

        return lax.fori_loop(0, ROWS // 64, step, state)

    def start_state():
        return (
            tuple(jnp.full((8, 128), NEG, jnp.float32) for _ in range(4)),
            tuple(jnp.zeros((8, 128), jnp.float32) for _ in range(4)),
        )

    def picked_ids(pair):
        side, source = place(hosted_mask(pair, blk), here)
        both = id_table[source]
        return jnp.where(side == 1, both[4:8, :], both[0:4, :])

    def finish_columns(pair, state):
        tops, sums = state
        for g in range(4):
            top = jnp.max(tops[g], axis=0, keepdims=True)
            total = jnp.sum(sums[g] * jnp.exp2(tops[g] - top), axis=0, keepdims=True)
            row = pair * 4 + g
            col_own[row : row + 1, :] = top + jnp.log2(total)

    for pair in range(2):
        loop(1, SPOTS, lambda k, pair=pair: deliver(pair, k).wait_recv())
        right_ids = picked_ids(pair)
        if pair == 0:
            to_sibling().wait_recv()
        state = start_state()
        state = tile(pair, 0, right_ids, state)
        state = tile(pair, 1, right_ids, state)
        if pair == 0:
            for i in range(PARTS):
                to_across(i).wait_recv()
                forward(i).start()
        state = tile(pair, 2, right_ids, state)
        if pair == 0:
            for i in range(PARTS):
                forward(i).wait_recv()
        state = tile(pair, 3, right_ids, state)
        finish_columns(pair, state)

    def col_copy(j):
        return remote(col_own, col_in.at[j], cola_s.at[j], cola_r.at[j], (intra, inter)[j])

    col_copy(0).start()
    col_copy(1).start()

    for j in (1, 2, 3, 0):
        for g in range(4):
            base = pl.ds(j * ROWS + g * 128, 128)
            first_top, second_top = row_max[0, base, :].T, row_max[1, base, :].T
            first_sum, second_sum = row_sum[0, base, :].T, row_sum[1, base, :].T
            top = jnp.max(jnp.maximum(first_top, second_top), axis=0, keepdims=True)
            total = jnp.sum(
                first_sum * jnp.exp2(first_top - top) + second_sum * jnp.exp2(second_top - top),
                axis=0,
                keepdims=True,
            )
            row_in[j, g : g + 1, :] = top + jnp.log2(total)

    def row_copy(j):
        return remote(
            row_in.at[j], row_in.at[3 + j], row_s.at[j], row_r.at[j], group[j - 1]
        )

    for j in range(1, 4):
        row_in[j, 4:8, :] = row_in[j, 0:4, :]
        row_copy(j).start()

    for j in range(2):
        col_copy(j).wait_recv()
    col_table[here, 0] = col_own[...]
    col_table[here, 1] = jnp.where(first_half, col_in[0], col_in[1])

    def col_spread(k):
        return remote(
            col_table.at[here], col_table.at[here], colb_s.at[k], colb_r.at[k], at_spot(k)
        )

    loop(1, SPOTS, lambda k: col_spread(k).start())
    loop(1, SPOTS, lambda k: col_spread(k).wait_recv())
    for j in range(1, 4):
        row_copy(j).wait_recv()

    terms = [row_in[0, 0:4, :]]
    for j in range(1, 4):
        terms.append(row_in[3 + j, 0:4, :])
    for pair in range(2):
        side, source = place(guest_mask(pair, blk), here)
        terms.append(col_table[source, side][pair * 4 : pair * 4 + 4, :])
    top = terms[0]
    for term in terms[1:]:
        top = jnp.maximum(top, term)
    total = jnp.exp2(terms[0] - top)
    for term in terms[1:]:
        total = total + jnp.exp2(term - top)
    out[...] = (top + jnp.log2(total)) * UNSCALE

    def sent(k):
        spread(k).wait_send()
        id_spread(k).wait_send()
        deliver(0, k).wait_send()
        deliver(1, k).wait_send()
        col_spread(k).wait_send()

    loop(1, SPOTS, sent)

    def handed(k):
        hand(k, 0).wait_send()
        hand(k, 1).wait_send()

    loop(0, SPOTS, handed)
    to_sibling().wait_send()
    for i in range(PARTS):
        to_across(i).wait_send()
        forward(i).wait_send()
    for j in range(1, 6):
        id_copy(j).wait_send()
    for j in range(1, 4):
        row_copy(j).wait_send()
    for j in range(2):
        col_copy(j).wait_send()


def shards(embeddings, doc_ids, plan):
    vmem = pl.BlockSpec(memory_space=pltpu.VMEM)
    sems = pltpu.SemaphoreType.DMA
    result = pl.pallas_call(
        kernel,
        out_shape=jax.ShapeDtypeStruct((4, 128), jnp.float32),
        in_specs=[pl.BlockSpec(memory_space=pltpu.SMEM), vmem, vmem],
        out_specs=vmem,
        scratch_shapes=[
            pltpu.VMEM((4, ROWS, D), jnp.bfloat16),
            pltpu.VMEM((2, SPOTS, CHUNK, D), jnp.bfloat16),
            pltpu.VMEM((2, SPOTS, CHUNK, D), jnp.bfloat16),
            pltpu.VMEM((2, SPOTS, CHUNK, D), jnp.bfloat16),
            pltpu.VMEM((4 * ROWS, 128), jnp.int32),
            pltpu.VMEM((6, 8, 128), jnp.int32),
            pltpu.VMEM((SPOTS, 8, 128), jnp.int32),
            pltpu.VMEM((ROWS, ROWS), jnp.float32),
            pltpu.VMEM((2, 4 * ROWS, 128), jnp.float32),
            pltpu.VMEM((2, 4 * ROWS, 128), jnp.float32),
            pltpu.VMEM((7, 8, 128), jnp.float32),
            pltpu.VMEM((8, 128), jnp.float32),
            pltpu.VMEM((2, 8, 128), jnp.float32),
            pltpu.VMEM((SPOTS, 2, 8, 128), jnp.float32),
            sems((SPOTS,)),
            sems((SPOTS,)),
            sems((2, SPOTS)),
            sems((2, SPOTS)),
            sems((2, SPOTS)),
            sems((2, SPOTS)),
            sems((1 + 2 * PARTS,)),
            sems((1 + 2 * PARTS,)),
            sems((6,)),
            sems((6,)),
            sems((SPOTS,)),
            sems((SPOTS,)),
            sems((4,)),
            sems((4,)),
            sems((2,)),
            sems((2,)),
            sems((SPOTS,)),
            sems((SPOTS,)),
        ],
        compiler_params=pltpu.CompilerParams(
            collective_id=0, has_side_effects=True, vmem_limit_bytes=56 * 2**20
        ),
        cost_estimate=pl.CostEstimate(
            flops=2 * 4 * ROWS * 2 * ROWS * D,
            bytes_accessed=ROWS * D * 2,
            transcendentals=2 * 4 * ROWS * 2 * ROWS,
        ),
        name="tournament",
    )(plan, embeddings, doc_ids.reshape(4, 128))
    return result.reshape(ROWS)


def solution(mesh):
    placed = (P(("blk", "rep"), None), P(("blk", "rep")), P())
    return jax.shard_map(
        shards, mesh=mesh, in_specs=placed, out_specs=P(("blk", "rep")), check_vma=False
    )
```

```python
import math

import jax
import jax.numpy as jnp
from jax import lax
from jax.experimental import pallas as pl
from jax.experimental.pallas import tpu as pltpu
from jax.sharding import PartitionSpec as P

MESH = pl.DeviceIdType.MESH
NEG = -1e30
SCALE = 256.0 * math.log2(math.e)
UNSCALE = math.log(2.0) / 256.0
ROWS = 512
BLOCKS = 32
SPOTS = 16
WAVES = 2
WAVE_ROWS = ROWS // WAVES
CHUNK = WAVE_ROWS // SPOTS
D = 1024
PARTS = 4
PIECE = ROWS // PARTS


def lowest_bit(value):
    return jnp.bitwise_and(value, -value)


def odd_bits(value):
    value = jnp.bitwise_xor(value, jnp.right_shift(value, 4))
    value = jnp.bitwise_xor(value, jnp.right_shift(value, 2))
    value = jnp.bitwise_xor(value, jnp.right_shift(value, 1))
    return jnp.bitwise_and(value, 1)


def chooser(first, second):
    common = jnp.bitwise_and(first, second)
    return jnp.where(
        common != 0,
        lowest_bit(common),
        jnp.bitwise_or(lowest_bit(first), lowest_bit(second)),
    )


def kernel(
    plan_in,
    emb_in,
    ids_in,
    out,
    plan,
    emb,
    left,
    held_first,
    held_second,
    outbox,
    right,
    left_ids,
    id_in,
    id_table,
    scores,
    row_max,
    row_sum,
    row_in,
    col_max,
    col_sum,
    col_own,
    col_in,
    col_table,
    load_s,
    one_s,
    one_r,
    rep_s,
    rep_r,
    two_s,
    two_r,
    own_s,
    own_r,
    ida_s,
    ida_r,
    idb_s,
    idb_r,
    row_s,
    row_r,
    cola_s,
    cola_r,
    colb_s,
    colb_r,
):
    held = (held_first, held_second)
    blk = lax.axis_index("blk")
    rep = lax.axis_index("rep")
    lo, z, y = blk // 16, (blk // 4) % 4, blk % 4
    hi, core = rep // 2, rep % 2
    here = z * 4 + y

    def at_spot(k):
        return (lo * 16 + ((z + k // 4) % 4) * 4 + (y + k % 4) % 4, rep)

    def spot_to(k):
        return ((z + k // 4) % 4) * 4 + (y + k % 4) % 4

    intra = ((1 - lo) * 16 + here, rep)
    inter = ((1 - lo) * 16 + here, (1 - hi) * 2 + core)
    sibling = (blk, hi * 2 + 1 - core)
    across = (blk, (1 - hi) * 2 + core)
    diagonal = (blk, (1 - hi) * 2 + 1 - core)

    def remote(src, dst, send, recv, device):
        return pltpu.make_async_remote_copy(
            src_ref=src,
            dst_ref=dst,
            send_sem=send,
            recv_sem=recv,
            device_id=device,
            device_id_type=MESH,
        )

    def loop(first, last, body):
        def step(k, carry):
            body(k)
            return carry

        lax.fori_loop(first, last, step, jnp.int32(0))

    barrier = pltpu.get_barrier_semaphore()
    for device in (intra, inter, sibling, across, diagonal):
        pl.semaphore_signal(barrier, inc=1, device_id=device, device_id_type=MESH)
    loop(
        1,
        SPOTS,
        lambda k: pl.semaphore_signal(barrier, inc=1, device_id=at_spot(k), device_id_type=MESH),
    )

    loads = [
        pltpu.make_async_copy(emb_in, emb, load_s.at[0]),
        pltpu.make_async_copy(plan_in, plan, load_s.at[1]),
        pltpu.make_async_copy(ids_in, id_in.at[0, 0:4], load_s.at[2]),
        pltpu.make_async_copy(ids_in, id_in.at[0, 4:8], load_s.at[3]),
    ]
    for load in loads:
        load.start()
    for load in loads:
        load.wait()

    def normalize(i):
        rows = pl.ds(pl.multiple_of(i * 64, 64), 64)
        wide = emb[rows, :].astype(jnp.float32)
        total = jnp.sum(wide * wide, axis=1, keepdims=True)
        left[0, rows, :] = (wide * lax.rsqrt(total + 1e-06)).astype(jnp.bfloat16)

    loop(0, ROWS // 64, normalize)
    pl.semaphore_wait(barrier, SPOTS - 1 + 5)

    def chunk(w, spot):
        return pl.ds(pl.multiple_of(w * WAVE_ROWS + spot * CHUNK, CHUNK), CHUNK)

    def spread(w, k):
        return remote(
            left.at[0, chunk(w, spot_to(k))],
            held[w].at[0, here],
            one_s.at[w, k],
            one_r.at[w, k],
            at_spot(k),
        )

    for w in range(WAVES):
        loop(1, SPOTS, lambda k, w=w: spread(w, k).start())
        held[w][0, here] = left[0, chunk(w, here), :]

    group = (sibling, across, diagonal, intra, inter)

    def id_copy(j):
        return remote(id_in.at[0], id_in.at[j], ida_s.at[j], ida_r.at[j], group[j - 1])

    for j in range(1, 6):
        id_copy(j).start()

    def to_sibling():
        return remote(left.at[0], left.at[1], own_s.at[0], own_r.at[0], sibling)

    def to_across(i):
        rows = pl.ds(i * PIECE, PIECE)
        return remote(
            left.at[0, rows], left.at[2, rows], own_s.at[1 + i], own_r.at[1 + i], across
        )

    def forward(i):
        rows = pl.ds(i * PIECE, PIECE)
        j = 1 + PARTS + i
        return remote(left.at[2, rows], left.at[3, rows], own_s.at[j], own_r.at[j], sibling)

    to_sibling().start()
    to_across(0).start()

    def hand(w, dz):
        from_z = (z + 4 - dz) % 4
        spots = pl.ds(from_z * 4, 4)
        side = (from_z + w) % 2
        return remote(
            held[w].at[0, spots],
            held[w].at[1, spots],
            rep_s.at[w, dz],
            rep_r.at[w, dz],
            ((1 - lo) * 16 + here, ((hi + side) % 2) * 2 + core),
        )

    for w in range(WAVES):
        for dz in (0, 1, 3, 2):
            for dy in range(4):
                if dz or dy:
                    spread(w, dz * 4 + dy).wait_recv()
            hand(w, dz).start()

    for j in range(1, 6):
        id_copy(j).wait_recv()
    id_table[here, 0:4, :] = id_in[0, 0:4, :]
    for w in range(WAVES):
        rows = slice(2 * w, 2 * w + 2)
        id_table[here, 4 + 2 * w : 6 + 2 * w, :] = jnp.where(
            (z + w) % 2 == 0, id_in[4, rows, :], id_in[5, rows, :]
        )

    def id_spread(k):
        return remote(
            id_table.at[here], id_table.at[here], idb_s.at[k], idb_r.at[k], at_spot(k)
        )

    loop(1, SPOTS, lambda k: id_spread(k).start())

    masks = [plan[r, 0] for r in range(4)]
    choosers = [chooser(masks[0], masks[1]), chooser(masks[2], masks[3])]

    def hosted_mask(pair, block):
        second = odd_bits(jnp.bitwise_and(block, choosers[pair]))
        return jnp.where(second == 1, masks[2 * pair + 1], masks[2 * pair])

    def guest_mask(pair, block):
        second = odd_bits(jnp.bitwise_and(block, choosers[pair]))
        return jnp.where(second == 1, masks[2 * pair], masks[2 * pair + 1])

    def place(mask, spot):
        return jnp.right_shift(mask, 4), jnp.bitwise_xor(spot, jnp.bitwise_and(mask, 15))

    def deliver(w, pair, k):
        return remote(
            outbox.at[w, pair, k],
            right.at[w, pair, here],
            two_s.at[w, pair, k],
            two_r.at[w, pair, k],
            at_spot(k),
        )

    def deliver_all(w, pair):
        def send_rows(k):
            spot = spot_to(k)
            side, source = place(hosted_mask(pair, lo * 16 + spot), spot)
            outbox[w, pair, k] = held[w][side, source]
            deliver(w, pair, k).start()

        loop(1, SPOTS, send_rows)
        side, source = place(hosted_mask(pair, blk), here)
        right[w, pair, here] = held[w][side, source]

    for w in range(WAVES):
        for dz in range(4):
            hand(w, dz).wait_recv()
        if w == WAVES - 1:
            for i in range(1, PARTS):
                to_across(i).start()
        for pair in range(2):
            deliver_all(w, pair)

    for j in range(4):
        for g in range(4):
            wide_ids = jnp.broadcast_to(id_in[j, g : g + 1, :], (128, 128))
            left_ids[pl.ds(j * ROWS + g * 128, 128), :] = wide_ids.T

    loop(1, SPOTS, lambda k: id_spread(k).wait_recv())

    def part_ids(w, pair):
        side, source = place(hosted_mask(pair, blk), here)
        both = id_table[source]
        return jnp.where(side == 1, both[4 + 2 * w : 6 + 2 * w, :], both[2 * w : 2 * w + 2, :])

    col_max[...] = jnp.full(col_max.shape, NEG, jnp.float32)
    col_sum[...] = jnp.zeros(col_sum.shape, jnp.float32)

    def tile(w, pair, slot, first, count):
        scores[0:count, :] = lax.dot_general(
            left[slot, first : first + count, :],
            right[w, pair].reshape(WAVE_ROWS, D),
            (((1,), (1,)), ((), ())),
            preferred_element_type=jnp.float32,
        )
        right_ids = part_ids(w, pair)
        part = w * 2 + pair

        def step(i, state):
            tops, sums = state
            rows = pl.ds(i * 64, 64)
            base = pl.ds(slot * ROWS + first + i * 64, 64)
            own_ids = left_ids[base, :]
            values = []
            for g in range(2):
                some = scores[rows, g * 128 : (g + 1) * 128] * SCALE
                values.append(jnp.where(own_ids == right_ids[g : g + 1, :], NEG, some))
            top = jnp.maximum(values[0], values[1])
            if part:
                older = row_max[base, :]
                top = jnp.maximum(top, older)
            total = jnp.exp2(values[0] - top) + jnp.exp2(values[1] - top)
            if part:
                total = total + row_sum[base, :] * jnp.exp2(older - top)
            row_max[base, :] = top
            row_sum[base, :] = total
            new_tops, new_sums = [], []
            for g in range(2):
                stack = values[g].reshape(8, 8, 128)
                new = jnp.maximum(tops[g], jnp.max(stack, axis=0))
                new_tops.append(new)
                new_sums.append(
                    sums[g] * jnp.exp2(tops[g] - new)
                    + jnp.sum(jnp.exp2(stack - new[None]), axis=0)
                )
            return tuple(new_tops), tuple(new_sums)

        state = (
            tuple(col_max[part, :, g * 128 : (g + 1) * 128] for g in range(2)),
            tuple(col_sum[part, :, g * 128 : (g + 1) * 128] for g in range(2)),
        )
        for i in range(count // 64):
            state = step(i, state)
        tops, sums = state
        for g in range(2):
            col_max[part, :, g * 128 : (g + 1) * 128] = tops[g]
            col_sum[part, :, g * 128 : (g + 1) * 128] = sums[g]

    def finish_columns(w, pair):
        part = w * 2 + pair
        tops = col_max[part]
        top = jnp.max(tops, axis=0, keepdims=True)
        total = jnp.sum(col_sum[part] * jnp.exp2(tops - top), axis=0, keepdims=True)
        result = top + jnp.log2(total)
        for g in range(2):
            row = pair * 4 + w * 2 + g
            col_own[row : row + 1, :] = result[:, g * 128 : (g + 1) * 128]

    def arrived(w, pair):
        loop(1, SPOTS, lambda k: deliver(w, pair, k).wait_recv())

    to_across(0).wait_recv()
    forward(0).start()
    to_sibling().wait_recv()
    half = ROWS // 2
    for pair in range(2):
        arrived(0, pair)
        tile(0, pair, 0, 0, ROWS)
        tile(0, pair, 1, 0, ROWS)
    to_across(1).wait_recv()
    forward(1).start()
    for pair in range(2):
        tile(0, pair, 2, 0, half)
    forward(0).wait_recv()
    forward(1).wait_recv()
    for pair in range(2):
        tile(0, pair, 3, 0, half)
    arrived(1, 0)
    tile(1, 0, 0, 0, ROWS)
    tile(1, 0, 1, 0, ROWS)
    tile(1, 0, 2, 0, half)
    tile(1, 0, 3, 0, half)
    for i in range(2, PARTS):
        to_across(i).wait_recv()
        forward(i).start()
    for w, pair in ((0, 0), (0, 1), (1, 0)):
        tile(w, pair, 2, half, half)
    for i in range(2, PARTS):
        forward(i).wait_recv()
    for w, pair in ((0, 0), (0, 1), (1, 0)):
        tile(w, pair, 3, half, half)
        finish_columns(w, pair)
    arrived(1, 1)
    for slot in (1, 2, 3, 0):
        tile(1, 1, slot, 0, ROWS)
    finish_columns(1, 1)

    def col_copy(j):
        return remote(col_own, col_in.at[j], cola_s.at[j], cola_r.at[j], (intra, inter)[j])

    col_copy(0).start()
    col_copy(1).start()

    def row_copy(j):
        return remote(
            row_in.at[j], row_in.at[3 + j], row_s.at[j], row_r.at[j], group[j - 1]
        )

    for j in (1, 2, 3, 0):
        for g in range(4):
            base = pl.ds(j * ROWS + g * 128, 128)
            tops = row_max[base, :].T
            top = jnp.max(tops, axis=0, keepdims=True)
            total = jnp.sum(row_sum[base, :].T * jnp.exp2(tops - top), axis=0, keepdims=True)
            row_in[j, g : g + 1, :] = top + jnp.log2(total)
        if j:
            row_in[j, 4:8, :] = row_in[j, 0:4, :]
            row_copy(j).start()

    for j in range(2):
        col_copy(j).wait_recv()
    col_table[here, 0] = col_own[...]
    for pair in range(2):
        source = place(hosted_mask(pair, (1 - lo) * 16 + here), here)[1]
        odd = jnp.bitwise_and(jnp.right_shift(source, 2), 1)
        for w in range(WAVES):
            rows = slice(pair * 4 + w * 2, pair * 4 + w * 2 + 2)
            col_table[here, 1, rows, :] = jnp.where(
                odd == w, col_in[0, rows, :], col_in[1, rows, :]
            )

    def col_spread(k):
        return remote(
            col_table.at[here], col_table.at[here], colb_s.at[k], colb_r.at[k], at_spot(k)
        )

    loop(1, SPOTS, lambda k: col_spread(k).start())
    loop(1, SPOTS, lambda k: col_spread(k).wait_recv())
    for j in range(1, 4):
        row_copy(j).wait_recv()

    terms = [row_in[0, 0:4, :]]
    for j in range(1, 4):
        terms.append(row_in[3 + j, 0:4, :])
    for pair in range(2):
        side, source = place(guest_mask(pair, blk), here)
        terms.append(col_table[source, side][pair * 4 : pair * 4 + 4, :])
    top = terms[0]
    for term in terms[1:]:
        top = jnp.maximum(top, term)
    total = jnp.exp2(terms[0] - top)
    for term in terms[1:]:
        total = total + jnp.exp2(term - top)
    out[...] = (top + jnp.log2(total)) * UNSCALE

    def sent(k):
        id_spread(k).wait_send()
        for w in range(WAVES):
            spread(w, k).wait_send()
            for pair in range(2):
                deliver(w, pair, k).wait_send()
        col_spread(k).wait_send()

    loop(1, SPOTS, sent)
    for w in range(WAVES):
        for dz in range(4):
            hand(w, dz).wait_send()
    to_sibling().wait_send()
    for i in range(PARTS):
        to_across(i).wait_send()
        forward(i).wait_send()
    for j in range(1, 6):
        id_copy(j).wait_send()
    for j in range(1, 4):
        row_copy(j).wait_send()
    for j in range(2):
        col_copy(j).wait_send()


def shards(embeddings, doc_ids, plan):
    sems = pltpu.SemaphoreType.DMA
    result = pl.pallas_call(
        kernel,
        out_shape=jax.ShapeDtypeStruct((4, 128), jnp.float32),
        in_specs=[pl.BlockSpec(memory_space=pl.ANY)] * 3,
        out_specs=pl.BlockSpec(memory_space=pltpu.VMEM),
        scratch_shapes=[
            pltpu.SMEM((4, BLOCKS), jnp.int32),
            pltpu.VMEM((ROWS, D), jnp.bfloat16),
            pltpu.VMEM((4, ROWS, D), jnp.bfloat16),
            pltpu.VMEM((2, SPOTS, CHUNK, D), jnp.bfloat16),
            pltpu.VMEM((2, SPOTS, CHUNK, D), jnp.bfloat16),
            pltpu.VMEM((WAVES, 2, SPOTS, CHUNK, D), jnp.bfloat16),
            pltpu.VMEM((WAVES, 2, SPOTS, CHUNK, D), jnp.bfloat16),
            pltpu.VMEM((4 * ROWS, 128), jnp.int32),
            pltpu.VMEM((6, 8, 128), jnp.int32),
            pltpu.VMEM((SPOTS, 8, 128), jnp.int32),
            pltpu.VMEM((ROWS, WAVE_ROWS), jnp.float32),
            pltpu.VMEM((4 * ROWS, 128), jnp.float32),
            pltpu.VMEM((4 * ROWS, 128), jnp.float32),
            pltpu.VMEM((7, 8, 128), jnp.float32),
            pltpu.VMEM((4, 8, WAVE_ROWS), jnp.float32),
            pltpu.VMEM((4, 8, WAVE_ROWS), jnp.float32),
            pltpu.VMEM((8, 128), jnp.float32),
            pltpu.VMEM((2, 8, 128), jnp.float32),
            pltpu.VMEM((SPOTS, 2, 8, 128), jnp.float32),
            sems((4,)),
            sems((WAVES, SPOTS)),
            sems((WAVES, SPOTS)),
            sems((WAVES, 4)),
            sems((WAVES, 4)),
            sems((WAVES, 2, SPOTS)),
            sems((WAVES, 2, SPOTS)),
            sems((1 + 2 * PARTS,)),
            sems((1 + 2 * PARTS,)),
            sems((6,)),
            sems((6,)),
            sems((SPOTS,)),
            sems((SPOTS,)),
            sems((4,)),
            sems((4,)),
            sems((2,)),
            sems((2,)),
            sems((SPOTS,)),
            sems((SPOTS,)),
        ],
        compiler_params=pltpu.CompilerParams(
            collective_id=0, has_side_effects=True, vmem_limit_bytes=56 * 2**20
        ),
        cost_estimate=pl.CostEstimate(
            flops=2 * 4 * ROWS * 2 * ROWS * D,
            bytes_accessed=ROWS * D * 2,
            transcendentals=2 * 4 * ROWS * 2 * ROWS,
        ),
        name="tournament",
    )(plan, embeddings, doc_ids.reshape(4, 128))
    return result.reshape(ROWS)


def solution(mesh):
    placed = (P(("blk", "rep"), None), P(("blk", "rep")), P())
    return jax.shard_map(
        shards, mesh=mesh, in_specs=placed, out_specs=P(("blk", "rep")), check_vma=False
    )
```

```python
import math

import jax
import jax.numpy as jnp
from jax import lax
from jax.experimental import pallas as pl
from jax.experimental.pallas import tpu as pltpu
from jax.sharding import PartitionSpec as P

MESH = pl.DeviceIdType.MESH
NEG = -1e30
SCALE = 256.0 * math.log2(math.e)
UNSCALE = math.log(2.0) / 256.0
ROWS = 512
BLOCKS = 32
SPOTS = 16
WAVES = 2
WAVE_ROWS = ROWS // WAVES
CHUNK = WAVE_ROWS // SPOTS
D = 1024
FAR_FIRST = (10, 6, 14, 9, 11, 2, 8, 5, 7, 13, 15, 1, 3, 4, 12, 0)
PARTS = 4
PIECE = ROWS // PARTS


def lowest_bit(value):
    return jnp.bitwise_and(value, -value)


def odd_bits(value):
    value = jnp.bitwise_xor(value, jnp.right_shift(value, 4))
    value = jnp.bitwise_xor(value, jnp.right_shift(value, 2))
    value = jnp.bitwise_xor(value, jnp.right_shift(value, 1))
    return jnp.bitwise_and(value, 1)


def chooser(first, second):
    common = jnp.bitwise_and(first, second)
    return jnp.where(
        common != 0,
        lowest_bit(common),
        jnp.bitwise_or(lowest_bit(first), lowest_bit(second)),
    )


def kernel(
    plan_in,
    emb_in,
    ids_in,
    out,
    plan,
    emb,
    left,
    held_first,
    held_second,
    outbox,
    right,
    left_ids,
    id_in,
    id_table,
    scores,
    row_max,
    row_sum,
    row_in,
    col_max,
    col_sum,
    col_own,
    col_table,
    load_s,
    one_s,
    one_r,
    rep_s,
    rep_r,
    two_s,
    two_r,
    own_s,
    own_r,
    ida_s,
    ida_r,
    idb_s,
    idb_r,
    row_s,
    row_r,
    colb_s,
    colb_r,
):
    held = (held_first, held_second)
    blk = lax.axis_index("blk")
    rep = lax.axis_index("rep")
    lo, z, y = blk // 16, (blk // 4) % 4, blk % 4
    hi, core = rep // 2, rep % 2
    here = z * 4 + y

    def at_spot(k):
        return (lo * 16 + ((z + k // 4) % 4) * 4 + (y + k % 4) % 4, rep)

    def spot_to(k):
        return ((z + k // 4) % 4) * 4 + (y + k % 4) % 4

    def beside(side, k):
        device_lo, device_hi = (lo + (side + 1) // 2) % 2, (hi + side // 2) % 2
        return (device_lo * 16 + spot_to(k), device_hi * 2 + core)

    intra = ((1 - lo) * 16 + here, rep)
    inter = ((1 - lo) * 16 + here, (1 - hi) * 2 + core)
    sibling = (blk, hi * 2 + 1 - core)
    across = (blk, (1 - hi) * 2 + core)
    diagonal = (blk, (1 - hi) * 2 + 1 - core)

    def remote(src, dst, send, recv, device):
        return pltpu.make_async_remote_copy(
            src_ref=src,
            dst_ref=dst,
            send_sem=send,
            recv_sem=recv,
            device_id=device,
            device_id_type=MESH,
        )

    def loop(first, last, body):
        def step(k, carry):
            body(k)
            return carry

        lax.fori_loop(first, last, step, jnp.int32(0))

    barrier = pltpu.get_barrier_semaphore()
    for device in (intra, inter, sibling, across, diagonal):
        pl.semaphore_signal(barrier, inc=1, device_id=device, device_id_type=MESH)
    loop(
        1,
        SPOTS,
        lambda k: pl.semaphore_signal(barrier, inc=1, device_id=at_spot(k), device_id_type=MESH),
    )

    loads = [
        pltpu.make_async_copy(emb_in, emb, load_s.at[0]),
        pltpu.make_async_copy(plan_in, plan, load_s.at[1]),
        pltpu.make_async_copy(ids_in, id_in.at[0, 0:4], load_s.at[2]),
        pltpu.make_async_copy(ids_in, id_in.at[0, 4:8], load_s.at[3]),
    ]
    for load in loads:
        load.start()
    for load in loads:
        load.wait()

    def normalize(i):
        rows = pl.ds(pl.multiple_of(i * 64, 64), 64)
        wide = emb[rows, :].astype(jnp.float32)
        total = jnp.sum(wide * wide, axis=1, keepdims=True)
        left[0, rows, :] = (wide * lax.rsqrt(total + 1e-06)).astype(jnp.bfloat16)

    loop(0, ROWS // 64, normalize)
    pl.semaphore_wait(barrier, SPOTS - 1 + 5)

    def chunk(w, spot):
        return pl.ds(pl.multiple_of(w * WAVE_ROWS + spot * CHUNK, CHUNK), CHUNK)

    def spread(w, k):
        return remote(
            left.at[0, chunk(w, spot_to(k))],
            held[w].at[0, here],
            one_s.at[w, k],
            one_r.at[w, k],
            at_spot(k),
        )

    for w in range(WAVES):
        loop(1, SPOTS, lambda k, w=w: spread(w, k).start())
        held[w][0, here] = left[0, chunk(w, here), :]

    group = (sibling, across, diagonal, intra, inter)

    def id_copy(j):
        return remote(id_in.at[0], id_in.at[j], ida_s.at[j], ida_r.at[j], group[j - 1])

    for j in range(1, 6):
        id_copy(j).start()

    def to_sibling():
        return remote(left.at[0], left.at[1], own_s.at[0], own_r.at[0], sibling)

    def to_across(i):
        rows = pl.ds(i * PIECE, PIECE)
        return remote(
            left.at[0, rows], left.at[2, rows], own_s.at[1 + i], own_r.at[1 + i], across
        )

    def forward(i):
        rows = pl.ds(i * PIECE, PIECE)
        j = 1 + PARTS + i
        return remote(left.at[2, rows], left.at[3, rows], own_s.at[j], own_r.at[j], sibling)

    to_sibling().start()
    to_across(0).start()

    def hand(w, dz):
        from_z = (z + 4 - dz) % 4
        spots = pl.ds(from_z * 4, 4)
        side = (from_z + w) % 2
        return remote(
            held[w].at[0, spots],
            held[w].at[1, spots],
            rep_s.at[w, dz],
            rep_r.at[w, dz],
            ((1 - lo) * 16 + here, ((hi + side) % 2) * 2 + core),
        )

    for w in range(WAVES):
        for dz in (0, 1, 3, 2):
            for dy in range(4):
                if dz or dy:
                    spread(w, dz * 4 + dy).wait_recv()
            hand(w, dz).start()

    for j in range(1, 6):
        id_copy(j).wait_recv()
    id_table[here, 0:4, :] = id_in[0, 0:4, :]
    for w in range(WAVES):
        rows = slice(2 * w, 2 * w + 2)
        id_table[here, 4 + 2 * w : 6 + 2 * w, :] = jnp.where(
            (z + w) % 2 == 0, id_in[4, rows, :], id_in[5, rows, :]
        )

    def id_spread(k):
        return remote(
            id_table.at[here], id_table.at[here], idb_s.at[k], idb_r.at[k], at_spot(k)
        )

    loop(1, SPOTS, lambda k: id_spread(k).start())

    masks = [plan[r, 0] for r in range(4)]
    choosers = [chooser(masks[0], masks[1]), chooser(masks[2], masks[3])]

    def hosted_mask(pair, block):
        second = odd_bits(jnp.bitwise_and(block, choosers[pair]))
        return jnp.where(second == 1, masks[2 * pair + 1], masks[2 * pair])

    def guest_mask(pair, block):
        second = odd_bits(jnp.bitwise_and(block, choosers[pair]))
        return jnp.where(second == 1, masks[2 * pair], masks[2 * pair + 1])

    def place(mask, spot):
        return jnp.right_shift(mask, 4), jnp.bitwise_xor(spot, jnp.bitwise_and(mask, 15))

    def deliver(w, pair, k):
        return remote(
            outbox.at[w, pair, k],
            right.at[w, pair, here],
            two_s.at[w, pair, k],
            two_r.at[w, pair, k],
            at_spot(k),
        )

    def deliver_all(w, pair):
        def send_rows(k):
            spot = spot_to(k)
            side, source = place(hosted_mask(pair, lo * 16 + spot), spot)
            outbox[w, pair, k] = held[w][side, source]
            deliver(w, pair, k).start()

        loop(1, SPOTS, send_rows)
        side, source = place(hosted_mask(pair, blk), here)
        right[w, pair, here] = held[w][side, source]

    for w in range(WAVES):
        for dz in range(4):
            hand(w, dz).wait_recv()
        if w == WAVES - 1:
            for i in range(1, PARTS):
                to_across(i).start()
        for pair in range(2):
            deliver_all(w, pair)

    for j in range(4):
        for g in range(4):
            wide_ids = jnp.broadcast_to(id_in[j, g : g + 1, :], (128, 128))
            left_ids[pl.ds(j * ROWS + g * 128, 128), :] = wide_ids.T

    loop(1, SPOTS, lambda k: id_spread(k).wait_recv())

    def part_ids(w, pair):
        side, source = place(hosted_mask(pair, blk), here)
        both = id_table[source]
        return jnp.where(side == 1, both[4 + 2 * w : 6 + 2 * w, :], both[2 * w : 2 * w + 2, :])

    col_max[...] = jnp.full(col_max.shape, NEG, jnp.float32)
    col_sum[...] = jnp.zeros(col_sum.shape, jnp.float32)

    def tile(w, pair, slot, first, count):
        scores[0:count, :] = lax.dot_general(
            left[slot, first : first + count, :],
            right[w, pair].reshape(WAVE_ROWS, D),
            (((1,), (1,)), ((), ())),
            preferred_element_type=jnp.float32,
        )
        right_ids = part_ids(w, pair)
        part = w * 2 + pair

        def step(i, state):
            tops, sums = state
            rows = pl.ds(i * 64, 64)
            base = pl.ds(slot * ROWS + first + i * 64, 64)
            own_ids = left_ids[base, :]
            values = []
            for g in range(2):
                some = scores[rows, g * 128 : (g + 1) * 128] * SCALE
                values.append(jnp.where(own_ids == right_ids[g : g + 1, :], NEG, some))
            top = jnp.maximum(values[0], values[1])
            if part:
                older = row_max[base, :]
                top = jnp.maximum(top, older)
            total = jnp.exp2(values[0] - top) + jnp.exp2(values[1] - top)
            if part:
                total = total + row_sum[base, :] * jnp.exp2(older - top)
            row_max[base, :] = top
            row_sum[base, :] = total
            new_tops, new_sums = [], []
            for g in range(2):
                stack = values[g].reshape(8, 8, 128)
                new = jnp.maximum(tops[g], jnp.max(stack, axis=0))
                new_tops.append(new)
                new_sums.append(
                    sums[g] * jnp.exp2(tops[g] - new)
                    + jnp.sum(jnp.exp2(stack - new[None]), axis=0)
                )
            return tuple(new_tops), tuple(new_sums)

        state = (
            tuple(col_max[part, :, g * 128 : (g + 1) * 128] for g in range(2)),
            tuple(col_sum[part, :, g * 128 : (g + 1) * 128] for g in range(2)),
        )
        for i in range(count // 64):
            state = step(i, state)
        tops, sums = state
        for g in range(2):
            col_max[part, :, g * 128 : (g + 1) * 128] = tops[g]
            col_sum[part, :, g * 128 : (g + 1) * 128] = sums[g]

    def finish_columns(w, pair):
        part = w * 2 + pair
        tops = col_max[part]
        top = jnp.max(tops, axis=0, keepdims=True)
        total = jnp.sum(col_sum[part] * jnp.exp2(tops - top), axis=0, keepdims=True)
        result = top + jnp.log2(total)
        for g in range(2):
            row = pair * 4 + w * 2 + g
            col_own[row : row + 1, :] = result[:, g * 128 : (g + 1) * 128]

    def arrived(w, pair):
        loop(1, SPOTS, lambda k: deliver(w, pair, k).wait_recv())

    to_across(0).wait_recv()
    forward(0).start()
    to_sibling().wait_recv()
    half = ROWS // 2
    for pair in range(2):
        arrived(0, pair)
        tile(0, pair, 0, 0, ROWS)
        tile(0, pair, 1, 0, ROWS)
    to_across(1).wait_recv()
    forward(1).start()
    for pair in range(2):
        tile(0, pair, 2, 0, half)
    forward(0).wait_recv()
    forward(1).wait_recv()
    for pair in range(2):
        tile(0, pair, 3, 0, half)
    for i in range(2, PARTS):
        to_across(i).wait_recv()
        forward(i).start()
    arrived(1, 0)
    tile(1, 0, 0, 0, ROWS)
    tile(1, 0, 1, 0, ROWS)
    tile(1, 0, 2, 0, half)
    tile(1, 0, 3, 0, half)
    for w, pair in ((0, 0), (0, 1), (1, 0)):
        tile(w, pair, 2, half, half)
    for i in range(2, PARTS):
        forward(i).wait_recv()
    for w, pair in ((0, 0), (0, 1), (1, 0)):
        tile(w, pair, 3, half, half)
        finish_columns(w, pair)
    arrived(1, 1)
    for slot in (1, 2, 3, 0):
        tile(1, 1, slot, 0, ROWS)
    finish_columns(1, 1)

    def col_spread(side, k):
        return remote(
            col_own,
            col_table.at[side, here],
            colb_s.at[side, k],
            colb_r.at[side, k],
            beside(side, k),
        )

    for k in FAR_FIRST:
        for side in (2, 1, 0):
            if side or k:
                col_spread(side, k).start()
    col_table[0, here] = col_own[...]

    def row_copy(j):
        return remote(
            row_in.at[j], row_in.at[3 + j], row_s.at[j], row_r.at[j], group[j - 1]
        )

    for j in (1, 2, 3, 0):
        for g in range(4):
            base = pl.ds(j * ROWS + g * 128, 128)
            tops = row_max[base, :].T
            top = jnp.max(tops, axis=0, keepdims=True)
            total = jnp.sum(row_sum[base, :].T * jnp.exp2(tops - top), axis=0, keepdims=True)
            row_in[j, g : g + 1, :] = top + jnp.log2(total)
        if j:
            row_in[j, 4:8, :] = row_in[j, 0:4, :]
            row_copy(j).start()

    def sent(k):
        id_spread(k).wait_send()
        for w in range(WAVES):
            spread(w, k).wait_send()
            for pair in range(2):
                deliver(w, pair, k).wait_send()

    loop(1, SPOTS, sent)
    for w in range(WAVES):
        for dz in range(4):
            hand(w, dz).wait_send()
    to_sibling().wait_send()
    for i in range(PARTS):
        to_across(i).wait_send()
        forward(i).wait_send()
    for j in range(1, 6):
        id_copy(j).wait_send()

    for side in range(3):
        loop(0 if side else 1, SPOTS, lambda k, side=side: col_spread(side, k).wait_recv())
    for j in range(1, 4):
        row_copy(j).wait_recv()

    for w in range(WAVES):
        rows = slice(2 * w, 2 * w + 2)
        terms = [row_in[0, rows, :]]
        for j in range(1, 4):
            terms.append(row_in[3 + j, rows, :])
        for pair in range(2):
            side, source = place(guest_mask(pair, blk), here)
            rows = slice(pair * 4 + 2 * w, pair * 4 + 2 * w + 2)
            near = col_table[0, source][rows, :]
            even, odd = col_table[1, source][rows, :], col_table[2, source][rows, :]
            terms.append(
                jnp.where(side == 1, jnp.where((z + w) % 2 == 0, even, odd), near)
            )
        top = terms[0]
        for term in terms[1:]:
            top = jnp.maximum(top, term)
        total = jnp.exp2(terms[0] - top)
        for term in terms[1:]:
            total = total + jnp.exp2(term - top)
        out[2 * w : 2 * w + 2, :] = (top + jnp.log2(total)) * UNSCALE

    for side in range(3):
        loop(0 if side else 1, SPOTS, lambda k, side=side: col_spread(side, k).wait_send())
    for j in range(1, 4):
        row_copy(j).wait_send()


def shards(embeddings, doc_ids, plan):
    sems = pltpu.SemaphoreType.DMA
    result = pl.pallas_call(
        kernel,
        out_shape=jax.ShapeDtypeStruct((4, 128), jnp.float32),
        in_specs=[pl.BlockSpec(memory_space=pl.ANY)] * 3,
        out_specs=pl.BlockSpec(memory_space=pltpu.VMEM),
        scratch_shapes=[
            pltpu.SMEM((4, BLOCKS), jnp.int32),
            pltpu.VMEM((ROWS, D), jnp.bfloat16),
            pltpu.VMEM((4, ROWS, D), jnp.bfloat16),
            pltpu.VMEM((2, SPOTS, CHUNK, D), jnp.bfloat16),
            pltpu.VMEM((2, SPOTS, CHUNK, D), jnp.bfloat16),
            pltpu.VMEM((WAVES, 2, SPOTS, CHUNK, D), jnp.bfloat16),
            pltpu.VMEM((WAVES, 2, SPOTS, CHUNK, D), jnp.bfloat16),
            pltpu.VMEM((4 * ROWS, 128), jnp.int32),
            pltpu.VMEM((6, 8, 128), jnp.int32),
            pltpu.VMEM((SPOTS, 8, 128), jnp.int32),
            pltpu.VMEM((ROWS, WAVE_ROWS), jnp.float32),
            pltpu.VMEM((4 * ROWS, 128), jnp.float32),
            pltpu.VMEM((4 * ROWS, 128), jnp.float32),
            pltpu.VMEM((7, 8, 128), jnp.float32),
            pltpu.VMEM((4, 8, WAVE_ROWS), jnp.float32),
            pltpu.VMEM((4, 8, WAVE_ROWS), jnp.float32),
            pltpu.VMEM((8, 128), jnp.float32),
            pltpu.VMEM((3, SPOTS, 8, 128), jnp.float32),
            sems((4,)),
            sems((WAVES, SPOTS)),
            sems((WAVES, SPOTS)),
            sems((WAVES, 4)),
            sems((WAVES, 4)),
            sems((WAVES, 2, SPOTS)),
            sems((WAVES, 2, SPOTS)),
            sems((1 + 2 * PARTS,)),
            sems((1 + 2 * PARTS,)),
            sems((6,)),
            sems((6,)),
            sems((SPOTS,)),
            sems((SPOTS,)),
            sems((4,)),
            sems((4,)),
            sems((3, SPOTS)),
            sems((3, SPOTS)),
        ],
        compiler_params=pltpu.CompilerParams(
            collective_id=0, has_side_effects=True, vmem_limit_bytes=56 * 2**20
        ),
        cost_estimate=pl.CostEstimate(
            flops=2 * 4 * ROWS * 2 * ROWS * D,
            bytes_accessed=ROWS * D * 2,
            transcendentals=2 * 4 * ROWS * 2 * ROWS,
        ),
        name="tournament",
    )(plan, embeddings, doc_ids.reshape(4, 128))
    return result.reshape(ROWS)


def solution(mesh):
    placed = (P(("blk", "rep"), None), P(("blk", "rep")), P())
    return jax.shard_map(
        shards, mesh=mesh, in_specs=placed, out_specs=P(("blk", "rep")), check_vma=False
    )
```

```python
import math

import jax
import jax.numpy as jnp
from jax import lax
from jax.experimental import pallas as pl
from jax.experimental.pallas import tpu as pltpu
from jax.sharding import PartitionSpec as P

MESH = pl.DeviceIdType.MESH
NEG = -1e30
SCALE = 256.0 * math.log2(math.e)
UNSCALE = math.log(2.0) / 256.0
ROWS = 512
BLOCKS = 32
SPOTS = 16
WAVES = 2
WAVE_ROWS = ROWS // WAVES
CHUNK = WAVE_ROWS // SPOTS
D = 1024
NEAR_FIRST = (3, 4, 12, 1, 8, 7, 15, 5, 13, 2, 11, 6, 9, 14, 10)
FAR_FIRST = (10, 6, 14, 9, 11, 2, 8, 5, 7, 13, 15, 1, 3, 4, 12, 0)
PARTS = 4
PIECE = ROWS // PARTS


def lowest_bit(value):
    return jnp.bitwise_and(value, -value)


def odd_bits(value):
    value = jnp.bitwise_xor(value, jnp.right_shift(value, 4))
    value = jnp.bitwise_xor(value, jnp.right_shift(value, 2))
    value = jnp.bitwise_xor(value, jnp.right_shift(value, 1))
    return jnp.bitwise_and(value, 1)


def chooser(first, second):
    common = jnp.bitwise_and(first, second)
    return jnp.where(
        common != 0,
        lowest_bit(common),
        jnp.bitwise_or(lowest_bit(first), lowest_bit(second)),
    )


def kernel(
    plan_in,
    emb_in,
    ids_in,
    out,
    plan,
    emb,
    left,
    held_first,
    held_second,
    outbox,
    right,
    left_ids,
    id_in,
    id_table,
    scores,
    row_max,
    row_sum,
    row_in,
    col_max,
    col_sum,
    col_own,
    col_table,
    load_s,
    one_s,
    one_r,
    rep_s,
    rep_r,
    two_s,
    two_r,
    own_s,
    own_r,
    ida_s,
    ida_r,
    idb_s,
    idb_r,
    row_s,
    row_r,
    colb_s,
    colb_r,
):
    held = (held_first, held_second)
    blk = lax.axis_index("blk")
    rep = lax.axis_index("rep")
    lo, z, y = blk // 16, (blk // 4) % 4, blk % 4
    hi, core = rep // 2, rep % 2
    here = z * 4 + y

    def at_spot(k):
        return (lo * 16 + ((z + k // 4) % 4) * 4 + (y + k % 4) % 4, rep)

    def spot_to(k):
        return ((z + k // 4) % 4) * 4 + (y + k % 4) % 4

    def beside(side, k):
        device_lo, device_hi = (lo + (side + 1) // 2) % 2, (hi + side // 2) % 2
        return (device_lo * 16 + spot_to(k), device_hi * 2 + core)

    intra = ((1 - lo) * 16 + here, rep)
    inter = ((1 - lo) * 16 + here, (1 - hi) * 2 + core)
    sibling = (blk, hi * 2 + 1 - core)
    across = (blk, (1 - hi) * 2 + core)
    diagonal = (blk, (1 - hi) * 2 + 1 - core)

    def remote(src, dst, send, recv, device):
        return pltpu.make_async_remote_copy(
            src_ref=src,
            dst_ref=dst,
            send_sem=send,
            recv_sem=recv,
            device_id=device,
            device_id_type=MESH,
        )

    def loop(first, last, body):
        def step(k, carry):
            body(k)
            return carry

        lax.fori_loop(first, last, step, jnp.int32(0))

    barrier = pltpu.get_barrier_semaphore()
    for device in (intra, inter, sibling, across, diagonal):
        pl.semaphore_signal(barrier, inc=1, device_id=device, device_id_type=MESH)
    loop(
        1,
        SPOTS,
        lambda k: pl.semaphore_signal(barrier, inc=1, device_id=at_spot(k), device_id_type=MESH),
    )

    loads = [
        pltpu.make_async_copy(emb_in, emb, load_s.at[0]),
        pltpu.make_async_copy(plan_in, plan, load_s.at[1]),
        pltpu.make_async_copy(ids_in, id_in.at[0, 0:4], load_s.at[2]),
        pltpu.make_async_copy(ids_in, id_in.at[0, 4:8], load_s.at[3]),
    ]
    for load in loads:
        load.start()
    for load in loads:
        load.wait()

    def normalize(i):
        rows = pl.ds(pl.multiple_of(i * 64, 64), 64)
        wide = emb[rows, :].astype(jnp.float32)
        total = jnp.sum(wide * wide, axis=1, keepdims=True)
        left[0, rows, :] = (wide * lax.rsqrt(total + 1e-06)).astype(jnp.bfloat16)

    loop(0, ROWS // 64, normalize)
    pl.semaphore_wait(barrier, SPOTS - 1 + 5)

    def chunk(w, spot):
        return pl.ds(pl.multiple_of(w * WAVE_ROWS + spot * CHUNK, CHUNK), CHUNK)

    def spread(w, k):
        return remote(
            left.at[0, chunk(w, spot_to(k))],
            held[w].at[0, here],
            one_s.at[w, k],
            one_r.at[w, k],
            at_spot(k),
        )

    for w in range(WAVES):
        loop(1, SPOTS, lambda k, w=w: spread(w, k).start())
        held[w][0, here] = left[0, chunk(w, here), :]

    group = (sibling, across, diagonal, intra, inter)

    def id_copy(j):
        return remote(id_in.at[0], id_in.at[j], ida_s.at[j], ida_r.at[j], group[j - 1])

    for j in range(1, 6):
        id_copy(j).start()

    def to_sibling():
        return remote(left.at[0], left.at[1], own_s.at[0], own_r.at[0], sibling)

    def to_across(i):
        rows = pl.ds(i * PIECE, PIECE)
        return remote(
            left.at[0, rows], left.at[2, rows], own_s.at[1 + i], own_r.at[1 + i], across
        )

    def forward(i):
        rows = pl.ds(i * PIECE, PIECE)
        j = 1 + PARTS + i
        return remote(left.at[2, rows], left.at[3, rows], own_s.at[j], own_r.at[j], sibling)

    to_sibling().start()
    to_across(0).start()

    def hand(w, dz):
        from_z = (z + 4 - dz) % 4
        spots = pl.ds(from_z * 4, 4)
        side = (from_z + w) % 2
        return remote(
            held[w].at[0, spots],
            held[w].at[1, spots],
            rep_s.at[w, dz],
            rep_r.at[w, dz],
            ((1 - lo) * 16 + here, ((hi + side) % 2) * 2 + core),
        )

    for w in range(WAVES):
        for dz in (0, 1, 3, 2):
            for dy in range(4):
                if dz or dy:
                    spread(w, dz * 4 + dy).wait_recv()
            hand(w, dz).start()

    for j in range(1, 6):
        id_copy(j).wait_recv()
    id_table[here, 0:4, :] = id_in[0, 0:4, :]
    for w in range(WAVES):
        rows = slice(2 * w, 2 * w + 2)
        id_table[here, 4 + 2 * w : 6 + 2 * w, :] = jnp.where(
            (z + w) % 2 == 0, id_in[4, rows, :], id_in[5, rows, :]
        )

    def id_spread(k):
        return remote(
            id_table.at[here], id_table.at[here], idb_s.at[k], idb_r.at[k], at_spot(k)
        )

    loop(1, SPOTS, lambda k: id_spread(k).start())

    masks = [plan[r, 0] for r in range(4)]
    choosers = [chooser(masks[0], masks[1]), chooser(masks[2], masks[3])]

    def hosted_mask(pair, block):
        second = odd_bits(jnp.bitwise_and(block, choosers[pair]))
        return jnp.where(second == 1, masks[2 * pair + 1], masks[2 * pair])

    def guest_mask(pair, block):
        second = odd_bits(jnp.bitwise_and(block, choosers[pair]))
        return jnp.where(second == 1, masks[2 * pair], masks[2 * pair + 1])

    def place(mask, spot):
        return jnp.right_shift(mask, 4), jnp.bitwise_xor(spot, jnp.bitwise_and(mask, 15))

    def deliver(w, pair, k):
        return remote(
            outbox.at[w, pair, k],
            right.at[w, pair, here],
            two_s.at[w, pair, k],
            two_r.at[w, pair, k],
            at_spot(k),
        )

    def deliver_all(w, pair):
        def send_rows(k):
            spot = spot_to(k)
            side, source = place(hosted_mask(pair, lo * 16 + spot), spot)
            outbox[w, pair, k] = held[w][side, source]
            deliver(w, pair, k).start()

        for k in NEAR_FIRST:
            send_rows(k)
        side, source = place(hosted_mask(pair, blk), here)
        right[w, pair, here] = held[w][side, source]

    for w in range(WAVES):
        for dz in range(4):
            hand(w, dz).wait_recv()
        for pair in range(2):
            if w == WAVES - 1:
                to_across(1 + pair).start()
            deliver_all(w, pair)
    to_across(3).start()

    for j in range(4):
        for g in range(4):
            wide_ids = jnp.broadcast_to(id_in[j, g : g + 1, :], (128, 128))
            left_ids[pl.ds(j * ROWS + g * 128, 128), :] = wide_ids.T

    loop(1, SPOTS, lambda k: id_spread(k).wait_recv())

    def part_ids(w, pair):
        side, source = place(hosted_mask(pair, blk), here)
        both = id_table[source]
        return jnp.where(side == 1, both[4 + 2 * w : 6 + 2 * w, :], both[2 * w : 2 * w + 2, :])

    col_max[...] = jnp.full(col_max.shape, NEG, jnp.float32)
    col_sum[...] = jnp.zeros(col_sum.shape, jnp.float32)

    def tile(w, pair, slot, first, count):
        scores[0:count, :] = lax.dot_general(
            left[slot, first : first + count, :],
            right[w, pair].reshape(WAVE_ROWS, D),
            (((1,), (1,)), ((), ())),
            preferred_element_type=jnp.float32,
        )
        right_ids = part_ids(w, pair)
        part = w * 2 + pair

        def step(i, state):
            tops, sums = state
            rows = pl.ds(i * 64, 64)
            base = pl.ds(slot * ROWS + first + i * 64, 64)
            own_ids = left_ids[base, :]
            values = []
            for g in range(2):
                some = scores[rows, g * 128 : (g + 1) * 128] * SCALE
                values.append(jnp.where(own_ids == right_ids[g : g + 1, :], NEG, some))
            top = jnp.maximum(values[0], values[1])
            if part:
                older = row_max[base, :]
                top = jnp.maximum(top, older)
            total = jnp.exp2(values[0] - top) + jnp.exp2(values[1] - top)
            if part:
                total = total + row_sum[base, :] * jnp.exp2(older - top)
            row_max[base, :] = top
            row_sum[base, :] = total
            new_tops, new_sums = [], []
            for g in range(2):
                stack = values[g].reshape(8, 8, 128)
                new = jnp.maximum(tops[g], jnp.max(stack, axis=0))
                new_tops.append(new)
                new_sums.append(
                    sums[g] * jnp.exp2(tops[g] - new)
                    + jnp.sum(jnp.exp2(stack - new[None]), axis=0)
                )
            return tuple(new_tops), tuple(new_sums)

        state = (
            tuple(col_max[part, :, g * 128 : (g + 1) * 128] for g in range(2)),
            tuple(col_sum[part, :, g * 128 : (g + 1) * 128] for g in range(2)),
        )
        for i in range(count // 64):
            state = step(i, state)
        tops, sums = state
        for g in range(2):
            col_max[part, :, g * 128 : (g + 1) * 128] = tops[g]
            col_sum[part, :, g * 128 : (g + 1) * 128] = sums[g]

    def finish_columns(w, pair):
        part = w * 2 + pair
        tops = col_max[part]
        top = jnp.max(tops, axis=0, keepdims=True)
        total = jnp.sum(col_sum[part] * jnp.exp2(tops - top), axis=0, keepdims=True)
        result = top + jnp.log2(total)
        for g in range(2):
            row = pair * 4 + w * 2 + g
            col_own[row : row + 1, :] = result[:, g * 128 : (g + 1) * 128]

    def arrived(w, pair):
        loop(1, SPOTS, lambda k: deliver(w, pair, k).wait_recv())

    to_across(0).wait_recv()
    forward(0).start()
    to_sibling().wait_recv()
    half = ROWS // 2
    for pair in range(2):
        arrived(0, pair)
        tile(0, pair, 0, 0, ROWS)
        tile(0, pair, 1, 0, ROWS)
    to_across(1).wait_recv()
    forward(1).start()
    for pair in range(2):
        tile(0, pair, 2, 0, half)
    forward(0).wait_recv()
    forward(1).wait_recv()
    for pair in range(2):
        tile(0, pair, 3, 0, half)
    for i in range(2, PARTS):
        to_across(i).wait_recv()
        forward(i).start()
    arrived(1, 0)
    tile(1, 0, 0, 0, ROWS)
    tile(1, 0, 1, 0, ROWS)
    tile(1, 0, 2, 0, half)
    tile(1, 0, 3, 0, half)
    for w, pair in ((0, 0), (0, 1), (1, 0)):
        tile(w, pair, 2, half, half)
    for i in range(2, PARTS):
        forward(i).wait_recv()
    for w, pair in ((0, 0), (0, 1), (1, 0)):
        tile(w, pair, 3, half, half)
        finish_columns(w, pair)
    arrived(1, 1)
    for slot in (1, 2, 3, 0):
        tile(1, 1, slot, 0, ROWS)
    finish_columns(1, 1)

    def col_spread(side, k):
        return remote(
            col_own,
            col_table.at[side, here],
            colb_s.at[side, k],
            colb_r.at[side, k],
            beside(side, k),
        )

    for k in FAR_FIRST:
        for side in (2, 1, 0):
            if side or k:
                col_spread(side, k).start()
    col_table[0, here] = col_own[...]

    def row_copy(j):
        return remote(
            row_in.at[j], row_in.at[3 + j], row_s.at[j], row_r.at[j], group[j - 1]
        )

    for j in (1, 2, 3, 0):
        for g in range(4):
            base = pl.ds(j * ROWS + g * 128, 128)
            tops = row_max[base, :].T
            top = jnp.max(tops, axis=0, keepdims=True)
            total = jnp.sum(row_sum[base, :].T * jnp.exp2(tops - top), axis=0, keepdims=True)
            row_in[j, g : g + 1, :] = top + jnp.log2(total)
        if j:
            row_in[j, 4:8, :] = row_in[j, 0:4, :]
            row_copy(j).start()

    def sent(k):
        id_spread(k).wait_send()
        for w in range(WAVES):
            spread(w, k).wait_send()
            for pair in range(2):
                deliver(w, pair, k).wait_send()

    loop(1, SPOTS, sent)
    for w in range(WAVES):
        for dz in range(4):
            hand(w, dz).wait_send()
    to_sibling().wait_send()
    for i in range(PARTS):
        to_across(i).wait_send()
        forward(i).wait_send()
    for j in range(1, 6):
        id_copy(j).wait_send()

    for side in range(3):
        loop(0 if side else 1, SPOTS, lambda k, side=side: col_spread(side, k).wait_recv())
    for j in range(1, 4):
        row_copy(j).wait_recv()

    for w in range(WAVES):
        rows = slice(2 * w, 2 * w + 2)
        terms = [row_in[0, rows, :]]
        for j in range(1, 4):
            terms.append(row_in[3 + j, rows, :])
        for pair in range(2):
            side, source = place(guest_mask(pair, blk), here)
            rows = slice(pair * 4 + 2 * w, pair * 4 + 2 * w + 2)
            near = col_table[0, source][rows, :]
            even, odd = col_table[1, source][rows, :], col_table[2, source][rows, :]
            terms.append(
                jnp.where(side == 1, jnp.where((z + w) % 2 == 0, even, odd), near)
            )
        top = terms[0]
        for term in terms[1:]:
            top = jnp.maximum(top, term)
        total = jnp.exp2(terms[0] - top)
        for term in terms[1:]:
            total = total + jnp.exp2(term - top)
        out[2 * w : 2 * w + 2, :] = (top + jnp.log2(total)) * UNSCALE

    for side in range(3):
        loop(0 if side else 1, SPOTS, lambda k, side=side: col_spread(side, k).wait_send())
    for j in range(1, 4):
        row_copy(j).wait_send()


def shards(embeddings, doc_ids, plan):
    sems = pltpu.SemaphoreType.DMA
    result = pl.pallas_call(
        kernel,
        out_shape=jax.ShapeDtypeStruct((4, 128), jnp.float32),
        in_specs=[pl.BlockSpec(memory_space=pl.ANY)] * 3,
        out_specs=pl.BlockSpec(memory_space=pltpu.VMEM),
        scratch_shapes=[
            pltpu.SMEM((4, BLOCKS), jnp.int32),
            pltpu.VMEM((ROWS, D), jnp.bfloat16),
            pltpu.VMEM((4, ROWS, D), jnp.bfloat16),
            pltpu.VMEM((2, SPOTS, CHUNK, D), jnp.bfloat16),
            pltpu.VMEM((2, SPOTS, CHUNK, D), jnp.bfloat16),
            pltpu.VMEM((WAVES, 2, SPOTS, CHUNK, D), jnp.bfloat16),
            pltpu.VMEM((WAVES, 2, SPOTS, CHUNK, D), jnp.bfloat16),
            pltpu.VMEM((4 * ROWS, 128), jnp.int32),
            pltpu.VMEM((6, 8, 128), jnp.int32),
            pltpu.VMEM((SPOTS, 8, 128), jnp.int32),
            pltpu.VMEM((ROWS, WAVE_ROWS), jnp.float32),
            pltpu.VMEM((4 * ROWS, 128), jnp.float32),
            pltpu.VMEM((4 * ROWS, 128), jnp.float32),
            pltpu.VMEM((7, 8, 128), jnp.float32),
            pltpu.VMEM((4, 8, WAVE_ROWS), jnp.float32),
            pltpu.VMEM((4, 8, WAVE_ROWS), jnp.float32),
            pltpu.VMEM((8, 128), jnp.float32),
            pltpu.VMEM((3, SPOTS, 8, 128), jnp.float32),
            sems((4,)),
            sems((WAVES, SPOTS)),
            sems((WAVES, SPOTS)),
            sems((WAVES, 4)),
            sems((WAVES, 4)),
            sems((WAVES, 2, SPOTS)),
            sems((WAVES, 2, SPOTS)),
            sems((1 + 2 * PARTS,)),
            sems((1 + 2 * PARTS,)),
            sems((6,)),
            sems((6,)),
            sems((SPOTS,)),
            sems((SPOTS,)),
            sems((4,)),
            sems((4,)),
            sems((3, SPOTS)),
            sems((3, SPOTS)),
        ],
        compiler_params=pltpu.CompilerParams(
            collective_id=0, has_side_effects=True, vmem_limit_bytes=56 * 2**20
        ),
        cost_estimate=pl.CostEstimate(
            flops=2 * 4 * ROWS * 2 * ROWS * D,
            bytes_accessed=ROWS * D * 2,
            transcendentals=2 * 4 * ROWS * 2 * ROWS,
        ),
        name="tournament",
    )(plan, embeddings, doc_ids.reshape(4, 128))
    return result.reshape(ROWS)


def solution(mesh):
    placed = (P(("blk", "rep"), None), P(("blk", "rep")), P())
    return jax.shard_map(
        shards, mesh=mesh, in_specs=placed, out_specs=P(("blk", "rep")), check_vma=False
    )
```

```python
import math

import jax
import jax.numpy as jnp
from jax import lax
from jax.experimental import pallas as pl
from jax.experimental.pallas import tpu as pltpu
from jax.sharding import PartitionSpec as P

MESH = pl.DeviceIdType.MESH
NEG = -1e30
SCALE = 256.0 * math.log2(math.e)
UNSCALE = math.log(2.0) / 256.0
ROWS = 512
BLOCKS = 32
SPOTS = 16
WAVES = 2
WAVE_ROWS = ROWS // WAVES
CHUNK = WAVE_ROWS // SPOTS
D = 1024
FAR_FIRST = (10, 6, 14, 9, 11, 2, 8, 5, 7, 13, 15, 1, 3, 4, 12, 0)
PARTS = 4
PIECE = ROWS // PARTS


def lowest_bit(value):
    return jnp.bitwise_and(value, -value)


def odd_bits(value):
    value = jnp.bitwise_xor(value, jnp.right_shift(value, 4))
    value = jnp.bitwise_xor(value, jnp.right_shift(value, 2))
    value = jnp.bitwise_xor(value, jnp.right_shift(value, 1))
    return jnp.bitwise_and(value, 1)


def chooser(first, second):
    common = jnp.bitwise_and(first, second)
    return jnp.where(
        common != 0,
        lowest_bit(common),
        jnp.bitwise_or(lowest_bit(first), lowest_bit(second)),
    )


def kernel(
    plan_in,
    emb_in,
    ids_in,
    out,
    plan,
    emb,
    left,
    held_first,
    held_second,
    outbox,
    right,
    left_ids,
    id_in,
    id_table,
    scores,
    row_max,
    row_sum,
    row_in,
    col_max,
    col_sum,
    col_own,
    col_table,
    load_s,
    one_s,
    one_r,
    rep_s,
    rep_r,
    two_s,
    two_r,
    own_s,
    own_r,
    ida_s,
    ida_r,
    idb_s,
    idb_r,
    row_s,
    row_r,
    colb_s,
    colb_r,
):
    held = (held_first, held_second)
    blk = lax.axis_index("blk")
    rep = lax.axis_index("rep")
    lo, z, y = blk // 16, (blk // 4) % 4, blk % 4
    hi, core = rep // 2, rep % 2
    here = z * 4 + y

    def at_spot(k):
        return (lo * 16 + ((z + k // 4) % 4) * 4 + (y + k % 4) % 4, rep)

    def spot_to(k):
        return ((z + k // 4) % 4) * 4 + (y + k % 4) % 4

    def beside(side, k):
        device_lo, device_hi = (lo + (side + 1) // 2) % 2, (hi + side // 2) % 2
        return (device_lo * 16 + spot_to(k), device_hi * 2 + core)

    intra = ((1 - lo) * 16 + here, rep)
    inter = ((1 - lo) * 16 + here, (1 - hi) * 2 + core)
    sibling = (blk, hi * 2 + 1 - core)
    across = (blk, (1 - hi) * 2 + core)
    diagonal = (blk, (1 - hi) * 2 + 1 - core)

    def remote(src, dst, send, recv, device):
        return pltpu.make_async_remote_copy(
            src_ref=src,
            dst_ref=dst,
            send_sem=send,
            recv_sem=recv,
            device_id=device,
            device_id_type=MESH,
        )

    def loop(first, last, body):
        def step(k, carry):
            body(k)
            return carry

        lax.fori_loop(first, last, step, jnp.int32(0))

    barrier = pltpu.get_barrier_semaphore()
    for device in (intra, inter, sibling, across, diagonal):
        pl.semaphore_signal(barrier, inc=1, device_id=device, device_id_type=MESH)
    loop(
        1,
        SPOTS,
        lambda k: pl.semaphore_signal(barrier, inc=1, device_id=at_spot(k), device_id_type=MESH),
    )

    loads = [
        pltpu.make_async_copy(emb_in, emb, load_s.at[0]),
        pltpu.make_async_copy(plan_in, plan, load_s.at[1]),
        pltpu.make_async_copy(ids_in, id_in.at[0, 0:4], load_s.at[2]),
        pltpu.make_async_copy(ids_in, id_in.at[0, 4:8], load_s.at[3]),
    ]
    for load in loads:
        load.start()
    for load in loads:
        load.wait()

    def normalize(i):
        rows = pl.ds(pl.multiple_of(i * 64, 64), 64)
        wide = emb[rows, :].astype(jnp.float32)
        total = jnp.sum(wide * wide, axis=1, keepdims=True)
        left[0, rows, :] = (wide * lax.rsqrt(total + 1e-06)).astype(jnp.bfloat16)

    loop(0, ROWS // 64, normalize)
    pl.semaphore_wait(barrier, SPOTS - 1 + 5)

    def chunk(w, spot):
        return pl.ds(pl.multiple_of(w * WAVE_ROWS + spot * CHUNK, CHUNK), CHUNK)

    def spread(w, k):
        return remote(
            left.at[0, chunk(w, spot_to(k))],
            held[w].at[0, here],
            one_s.at[w, k],
            one_r.at[w, k],
            at_spot(k),
        )

    for w in range(WAVES):
        loop(1, SPOTS, lambda k, w=w: spread(w, k).start())
        held[w][0, here] = left[0, chunk(w, here), :]

    group = (sibling, across, diagonal, intra, inter)

    def id_copy(j):
        return remote(id_in.at[0], id_in.at[j], ida_s.at[j], ida_r.at[j], group[j - 1])

    for j in range(1, 6):
        id_copy(j).start()

    def to_sibling():
        return remote(left.at[0], left.at[1], own_s.at[0], own_r.at[0], sibling)

    def to_across(i):
        rows = pl.ds(i * PIECE, PIECE)
        return remote(
            left.at[0, rows], left.at[2, rows], own_s.at[1 + i], own_r.at[1 + i], across
        )

    def forward(i):
        rows = pl.ds(i * PIECE, PIECE)
        j = 1 + PARTS + i
        return remote(left.at[2, rows], left.at[3, rows], own_s.at[j], own_r.at[j], sibling)

    to_sibling().start()
    to_across(0).start()

    def hand(w, dz):
        from_z = (z + 4 - dz) % 4
        spots = pl.ds(from_z * 4, 4)
        side = (from_z + w) % 2
        return remote(
            held[w].at[0, spots],
            held[w].at[1, spots],
            rep_s.at[w, dz],
            rep_r.at[w, dz],
            ((1 - lo) * 16 + here, ((hi + side) % 2) * 2 + core),
        )

    for w in range(WAVES):
        for dz in (0, 1, 3, 2):
            for dy in range(4):
                if dz or dy:
                    spread(w, dz * 4 + dy).wait_recv()
            hand(w, dz).start()

    for j in range(1, 6):
        id_copy(j).wait_recv()
    id_table[here, 0:4, :] = id_in[0, 0:4, :]
    for w in range(WAVES):
        rows = slice(2 * w, 2 * w + 2)
        id_table[here, 4 + 2 * w : 6 + 2 * w, :] = jnp.where(
            (z + w) % 2 == 0, id_in[4, rows, :], id_in[5, rows, :]
        )

    def id_spread(k):
        return remote(
            id_table.at[here], id_table.at[here], idb_s.at[k], idb_r.at[k], at_spot(k)
        )

    loop(1, SPOTS, lambda k: id_spread(k).start())

    masks = [plan[r, 0] for r in range(4)]
    choosers = [chooser(masks[0], masks[1]), chooser(masks[2], masks[3])]

    def hosted_mask(pair, block):
        second = odd_bits(jnp.bitwise_and(block, choosers[pair]))
        return jnp.where(second == 1, masks[2 * pair + 1], masks[2 * pair])

    def guest_mask(pair, block):
        second = odd_bits(jnp.bitwise_and(block, choosers[pair]))
        return jnp.where(second == 1, masks[2 * pair], masks[2 * pair + 1])

    def place(mask, spot):
        return jnp.right_shift(mask, 4), jnp.bitwise_xor(spot, jnp.bitwise_and(mask, 15))

    def deliver(w, pair, k):
        return remote(
            outbox.at[w, pair, k],
            right.at[w, pair, here],
            two_s.at[w, pair, k],
            two_r.at[w, pair],
            at_spot(k),
        )

    def deliver_all(w, pair):
        def send_rows(k):
            spot = spot_to(k)
            side, source = place(hosted_mask(pair, lo * 16 + spot), spot)
            outbox[w, pair, k] = held[w][side, source]
            deliver(w, pair, k).start()

        loop(1, SPOTS, send_rows)
        side, source = place(hosted_mask(pair, blk), here)
        right[w, pair, here] = held[w][side, source]

    for w in range(WAVES):
        for dz in range(4):
            hand(w, dz).wait_recv()
        if w == WAVES - 1:
            for i in range(1, PARTS):
                to_across(i).start()
        for pair in range(2):
            deliver_all(w, pair)

    for j in range(4):
        for g in range(4):
            wide_ids = jnp.broadcast_to(id_in[j, g : g + 1, :], (128, 128))
            left_ids[pl.ds(j * ROWS + g * 128, 128), :] = wide_ids.T

    loop(1, SPOTS, lambda k: id_spread(k).wait_recv())

    def part_ids(w, pair):
        side, source = place(hosted_mask(pair, blk), here)
        both = id_table[source]
        return jnp.where(side == 1, both[4 + 2 * w : 6 + 2 * w, :], both[2 * w : 2 * w + 2, :])

    col_max[...] = jnp.full(col_max.shape, NEG, jnp.float32)
    col_sum[...] = jnp.zeros(col_sum.shape, jnp.float32)

    def tile(w, pair, slot, first, count):
        scores[0:count, :] = lax.dot_general(
            left[slot, first : first + count, :],
            right[w, pair].reshape(WAVE_ROWS, D),
            (((1,), (1,)), ((), ())),
            preferred_element_type=jnp.float32,
        )
        right_ids = part_ids(w, pair)
        part = w * 2 + pair

        def step(i, state):
            tops, sums = state
            rows = pl.ds(i * 64, 64)
            base = pl.ds(slot * ROWS + first + i * 64, 64)
            own_ids = left_ids[base, :]
            values = []
            for g in range(2):
                some = scores[rows, g * 128 : (g + 1) * 128] * SCALE
                values.append(jnp.where(own_ids == right_ids[g : g + 1, :], NEG, some))
            top = jnp.maximum(values[0], values[1])
            if part:
                older = row_max[base, :]
                top = jnp.maximum(top, older)
            total = jnp.exp2(values[0] - top) + jnp.exp2(values[1] - top)
            if part:
                total = total + row_sum[base, :] * jnp.exp2(older - top)
            row_max[base, :] = top
            row_sum[base, :] = total
            new_tops, new_sums = [], []
            for g in range(2):
                stack = values[g].reshape(8, 8, 128)
                new = jnp.maximum(tops[g], jnp.max(stack, axis=0))
                new_tops.append(new)
                new_sums.append(
                    sums[g] * jnp.exp2(tops[g] - new)
                    + jnp.sum(jnp.exp2(stack - new[None]), axis=0)
                )
            return tuple(new_tops), tuple(new_sums)

        state = (
            tuple(col_max[part, :, g * 128 : (g + 1) * 128] for g in range(2)),
            tuple(col_sum[part, :, g * 128 : (g + 1) * 128] for g in range(2)),
        )
        for i in range(count // 64):
            state = step(i, state)
        tops, sums = state
        for g in range(2):
            col_max[part, :, g * 128 : (g + 1) * 128] = tops[g]
            col_sum[part, :, g * 128 : (g + 1) * 128] = sums[g]

    def finish_columns(w, pair):
        part = w * 2 + pair
        tops = col_max[part]
        top = jnp.max(tops, axis=0, keepdims=True)
        total = jnp.sum(col_sum[part] * jnp.exp2(tops - top), axis=0, keepdims=True)
        result = top + jnp.log2(total)
        for g in range(2):
            row = pair * 4 + w * 2 + g
            col_own[row : row + 1, :] = result[:, g * 128 : (g + 1) * 128]

    def arrived(w, pair):
        some = right.at[w, pair, pl.ds(0, SPOTS - 1)]
        remote(some, some, two_s.at[w, pair, 0], two_r.at[w, pair], at_spot(1)).wait_recv()

    to_across(0).wait_recv()
    forward(0).start()
    to_sibling().wait_recv()
    half = ROWS // 2
    for pair in range(2):
        arrived(0, pair)
        tile(0, pair, 0, 0, ROWS)
        tile(0, pair, 1, 0, ROWS)
    to_across(1).wait_recv()
    forward(1).start()
    for pair in range(2):
        tile(0, pair, 2, 0, half)
    forward(0).wait_recv()
    forward(1).wait_recv()
    for pair in range(2):
        tile(0, pair, 3, 0, half)
    for i in range(2, PARTS):
        to_across(i).wait_recv()
        forward(i).start()
    arrived(1, 0)
    tile(1, 0, 0, 0, ROWS)
    tile(1, 0, 1, 0, ROWS)
    tile(1, 0, 2, 0, half)
    tile(1, 0, 3, 0, half)
    for w, pair in ((0, 0), (0, 1), (1, 0)):
        tile(w, pair, 2, half, half)
    for i in range(2, PARTS):
        forward(i).wait_recv()
    for w, pair in ((0, 0), (0, 1), (1, 0)):
        tile(w, pair, 3, half, half)
        finish_columns(w, pair)
    arrived(1, 1)
    for slot in (1, 2, 3, 0):
        tile(1, 1, slot, 0, ROWS)
    finish_columns(1, 1)

    def col_spread(side, k):
        return remote(
            col_own,
            col_table.at[side, here],
            colb_s.at[side, k],
            colb_r.at[side],
            beside(side, k),
        )

    for k in FAR_FIRST:
        for side in (2, 1, 0):
            if side or k:
                col_spread(side, k).start()
    col_table[0, here] = col_own[...]

    def row_copy(j):
        return remote(
            row_in.at[j], row_in.at[3 + j], row_s.at[j], row_r.at[j], group[j - 1]
        )

    for j in (1, 2, 3, 0):
        for g in range(4):
            base = pl.ds(j * ROWS + g * 128, 128)
            tops = row_max[base, :].T
            top = jnp.max(tops, axis=0, keepdims=True)
            total = jnp.sum(row_sum[base, :].T * jnp.exp2(tops - top), axis=0, keepdims=True)
            row_in[j, g : g + 1, :] = top + jnp.log2(total)
        if j:
            row_in[j, 4:8, :] = row_in[j, 0:4, :]
            row_copy(j).start()

    def sent(k):
        id_spread(k).wait_send()
        for w in range(WAVES):
            spread(w, k).wait_send()
            for pair in range(2):
                deliver(w, pair, k).wait_send()

    loop(1, SPOTS, sent)
    for w in range(WAVES):
        for dz in range(4):
            hand(w, dz).wait_send()
    to_sibling().wait_send()
    for i in range(PARTS):
        to_across(i).wait_send()
        forward(i).wait_send()
    for j in range(1, 6):
        id_copy(j).wait_send()

    for side in range(3):
        some = col_table.at[side, pl.ds(0, SPOTS if side else SPOTS - 1)]
        remote(some, some, colb_s.at[side, 0], colb_r.at[side], at_spot(1)).wait_recv()
    for j in range(1, 4):
        row_copy(j).wait_recv()

    for w in range(WAVES):
        rows = slice(2 * w, 2 * w + 2)
        terms = [row_in[0, rows, :]]
        for j in range(1, 4):
            terms.append(row_in[3 + j, rows, :])
        for pair in range(2):
            side, source = place(guest_mask(pair, blk), here)
            rows = slice(pair * 4 + 2 * w, pair * 4 + 2 * w + 2)
            near = col_table[0, source][rows, :]
            even, odd = col_table[1, source][rows, :], col_table[2, source][rows, :]
            terms.append(
                jnp.where(side == 1, jnp.where((z + w) % 2 == 0, even, odd), near)
            )
        top = terms[0]
        for term in terms[1:]:
            top = jnp.maximum(top, term)
        total = jnp.exp2(terms[0] - top)
        for term in terms[1:]:
            total = total + jnp.exp2(term - top)
        out[2 * w : 2 * w + 2, :] = (top + jnp.log2(total)) * UNSCALE

    for side in range(3):
        loop(0 if side else 1, SPOTS, lambda k, side=side: col_spread(side, k).wait_send())
    for j in range(1, 4):
        row_copy(j).wait_send()


def shards(embeddings, doc_ids, plan):
    sems = pltpu.SemaphoreType.DMA
    result = pl.pallas_call(
        kernel,
        out_shape=jax.ShapeDtypeStruct((4, 128), jnp.float32),
        in_specs=[pl.BlockSpec(memory_space=pl.ANY)] * 3,
        out_specs=pl.BlockSpec(memory_space=pltpu.VMEM),
        scratch_shapes=[
            pltpu.SMEM((4, BLOCKS), jnp.int32),
            pltpu.VMEM((ROWS, D), jnp.bfloat16),
            pltpu.VMEM((4, ROWS, D), jnp.bfloat16),
            pltpu.VMEM((2, SPOTS, CHUNK, D), jnp.bfloat16),
            pltpu.VMEM((2, SPOTS, CHUNK, D), jnp.bfloat16),
            pltpu.VMEM((WAVES, 2, SPOTS, CHUNK, D), jnp.bfloat16),
            pltpu.VMEM((WAVES, 2, SPOTS, CHUNK, D), jnp.bfloat16),
            pltpu.VMEM((4 * ROWS, 128), jnp.int32),
            pltpu.VMEM((6, 8, 128), jnp.int32),
            pltpu.VMEM((SPOTS, 8, 128), jnp.int32),
            pltpu.VMEM((ROWS, WAVE_ROWS), jnp.float32),
            pltpu.VMEM((4 * ROWS, 128), jnp.float32),
            pltpu.VMEM((4 * ROWS, 128), jnp.float32),
            pltpu.VMEM((7, 8, 128), jnp.float32),
            pltpu.VMEM((4, 8, WAVE_ROWS), jnp.float32),
            pltpu.VMEM((4, 8, WAVE_ROWS), jnp.float32),
            pltpu.VMEM((8, 128), jnp.float32),
            pltpu.VMEM((3, SPOTS, 8, 128), jnp.float32),
            sems((4,)),
            sems((WAVES, SPOTS)),
            sems((WAVES, SPOTS)),
            sems((WAVES, 4)),
            sems((WAVES, 4)),
            sems((WAVES, 2, SPOTS)),
            sems((WAVES, 2)),
            sems((1 + 2 * PARTS,)),
            sems((1 + 2 * PARTS,)),
            sems((6,)),
            sems((6,)),
            sems((SPOTS,)),
            sems((SPOTS,)),
            sems((4,)),
            sems((4,)),
            sems((3, SPOTS)),
            sems((3,)),
        ],
        compiler_params=pltpu.CompilerParams(
            collective_id=0, has_side_effects=True, vmem_limit_bytes=56 * 2**20
        ),
        cost_estimate=pl.CostEstimate(
            flops=2 * 4 * ROWS * 2 * ROWS * D,
            bytes_accessed=ROWS * D * 2,
            transcendentals=2 * 4 * ROWS * 2 * ROWS,
        ),
        name="tournament",
    )(plan, embeddings, doc_ids.reshape(4, 128))
    return result.reshape(ROWS)


def solution(mesh):
    placed = (P(("blk", "rep"), None), P(("blk", "rep")), P())
    return jax.shard_map(
        shards, mesh=mesh, in_specs=placed, out_specs=P(("blk", "rep")), check_vma=False
    )
```
